32 devices in a mesh: row: 4 (over y, x), col: 8 (over z, core).
Axes of the slice: x: 2, y: 2, z: 4, core: 2. Of those that a mesh axis runs over, the one named last changes fastest.
Arguments:
- queries: bfloat16 [4096, 768], P(('row', 'col')), may hold values from -8 to 8
- tools: bfloat16 [6144, 768], P(('col', 'row')), may hold values from -8 to 8
- query_mass: float32 [4096], P('row'), may hold values from 0.5 to 5
- tool_mass: float32 [6144], P('col'), may hold values from 0.5 to 5
Outputs:
- mapped_queries: bfloat16 [4096, 768], P(('row', 'col'))
- query_potential: float32 [4096], P('row')
- tool_potential: float32 [6144], P('col')
The draws below stay inside these ranges and needn't reach their ends.
All inputs are finite; a program needn't handle non-finite values.
Results may differ from the reference program's by a relative error of at most 0.0025.
Values may be sent and summed in bfloat16 or wider, within the bound.
No kernel may reach another device: no remote copies, remote signals or barrier semaphores. Data moves between devices by JAX's collectives and lax.ppermute only.
A program may use at most 64 MiB of HBM per device.

```python
import math
import jax
import jax.numpy as jnp
from jax import lax

D = 768
QR_DEV = 1024
ITERS = 3
NQ = 4096
NT = 6144


def embed_draw(key):
    query_key = jax.random.fold_in(key, 101)
    tool_key = jax.random.fold_in(key, 202)
    sign_key = jax.random.fold_in(key, 606)
    half_width = D // 2
    sign_pattern = (jax.random.randint(sign_key, (D,), 0, 2) * 2 - 1).astype(jnp.float32)
    first_half = jnp.arange(D) < half_width
    query_common = jnp.where(first_half, sign_pattern, 0.0)
    tool_common = jnp.where(first_half, 0.0, sign_pattern)
    queries = jax.random.truncated_normal(query_key, -6.0, 6.0, (NQ, D), jnp.float32)
    tools = jax.random.truncated_normal(tool_key, -6.0, 6.0, (NT, D), jnp.float32)
    queries = queries + query_common[None, :]
    tools = tools + tool_common[None, :]
    for block_index in (1, 3, 5):
        far_query = block_index * (NQ // 6) + NQ // 12
        far_tool = block_index * (NT // 6) + NT // 12
        queries = queries.at[far_query].set(jnp.where(first_half, queries[far_query], -8.0 * tool_common))
        tools = tools.at[far_tool].set(jnp.where(first_half, -8.0 * query_common, tools[far_tool]))
    return (queries, tools)


def draw_queries(key, part):
    return embed_draw(key)[0].astype(jnp.bfloat16)


def draw_tools(key, part):
    return embed_draw(key)[1].astype(jnp.bfloat16)


def draw_query_mass(key, part):
    position = jnp.arange(NQ, dtype=jnp.float32) / NQ
    noise = jax.random.uniform(jax.random.fold_in(key, 404), (NQ,), jnp.float32, -0.5, 0.5)
    return jnp.exp(noise) * jnp.exp(position * 1.0986123)


def draw_tool_mass(key, part):
    position = jnp.arange(NT, dtype=jnp.float32) / NT
    noise = jax.random.uniform(jax.random.fold_in(key, 505), (NT,), jnp.float32, -0.5, 0.5)
    return jnp.exp(noise) * jnp.exp(position * 1.0986123)


def setup_inputs(seed: int = 0) -> dict:
    seeds = jax.random.split(jax.random.key(seed), 5)
    queries = draw_queries(jax.random.fold_in(seeds[4], 71), 0)
    tools = draw_tools(jax.random.fold_in(seeds[4], 71), 0)
    query_mass = draw_query_mass(jax.random.fold_in(seeds[4], 71), 0)
    tool_mass = draw_tool_mass(jax.random.fold_in(seeds[4], 71), 0)
    return {"queries": queries, "tools": tools, "query_mass": query_mass, "tool_mass": tool_mass}


EPSILON = 0.5

def cost_block(query_block, tools):
    products = jnp.dot(query_block, tools.T, preferred_element_type=jnp.float32)
    return products * (-1.0 / math.sqrt(D))

def reference(queries, tools, query_mass, tool_mass):
    query_blocks = queries.reshape(NQ // QR_DEV, QR_DEV, D)
    log_query = jnp.log(query_mass)
    log_tool = jnp.log(tool_mass)

    def row_pass(tool_potential):

        def one_block(query_block):
            scores = (tool_potential[None, :] - cost_block(query_block, tools)) / EPSILON
            maxima = lax.optimization_barrier(jnp.max(scores, axis=1))
            return maxima + jnp.log(lax.optimization_barrier(jnp.sum(jnp.exp(scores - maxima[:, None]), axis=1)))
        return lax.map(one_block, query_blocks).reshape(NQ)

    def column_pass(query_potential):
        potential_blocks = query_potential.reshape(NQ // QR_DEV, QR_DEV)

        def advance(running, element):
            query_block, potential_block = element
            scores = (potential_block[:, None] - cost_block(query_block, tools)) / EPSILON
            highest = jnp.maximum(running[0], lax.optimization_barrier(jnp.max(scores, axis=0)))
            summed = running[1] * jnp.exp(running[0] - highest) + lax.optimization_barrier(jnp.sum(jnp.exp(scores - highest[None, :]), axis=0))
            return ((highest, summed), None)
        start_state = (jnp.full((NT,), -jnp.inf, jnp.float32), jnp.zeros((NT,), jnp.float32))
        final_state, unused = lax.scan(advance, start_state, (query_blocks, potential_blocks))
        return final_state[0] + jnp.log(final_state[1])
    tool_potential = jnp.zeros((NT,), jnp.float32)
    query_potential = jnp.zeros((NQ,), jnp.float32)
    for sweep in range(ITERS):
        query_potential = EPSILON * log_query - EPSILON * row_pass(tool_potential)
        tool_potential = EPSILON * log_tool - EPSILON * column_pass(query_potential)

    def map_block(query_block):
        scores = (tool_potential[None, :] - cost_block(query_block, tools)) / EPSILON
        peaks = lax.optimization_barrier(jnp.max(scores, axis=1))
        exps = jnp.exp(scores - peaks[:, None])
        totals = lax.optimization_barrier(jnp.sum(exps, axis=1))
        weights = exps.astype(jnp.bfloat16)
        summed = jnp.dot(weights, tools, preferred_element_type=jnp.float32)
        return (summed / totals[:, None]).astype(jnp.bfloat16)
    mapped_queries = lax.map(map_block, query_blocks).reshape(NQ, D)
    return (mapped_queries, query_potential, tool_potential)
```

```python
import math

import jax
import jax.numpy as jnp
from jax import lax
from jax.sharding import PartitionSpec as P

ITERS = 3
EPSILON = 0.5
LOG2E = 1.0 / math.log(2.0)


def swap(x, axis, k):
    n = lax.axis_size(axis)
    return lax.ppermute(x, axis, [(i, i ^ k) for i in range(n)])


def place(blocks, index):
    whole = jnp.zeros((len(blocks),) + blocks[0].shape, blocks[0].dtype)
    for k, block in enumerate(blocks):
        whole = lax.dynamic_update_index_in_dim(whole, block, index ^ k, 0)
    return whole


def lse_of(parts):
    highest = parts[0]
    for part in parts[1:]:
        highest = jnp.maximum(highest, part)
    total = jnp.exp2(parts[0] - highest)
    for part in parts[1:]:
        total = total + jnp.exp2(part - highest)
    return highest + jnp.log2(total)


def local_lse(scores, axis):
    highest = jnp.max(scores, axis=axis, keepdims=True)
    total = jnp.sum(jnp.exp2(scores - highest), axis=axis)
    return jnp.squeeze(highest, axis) + jnp.log2(total)


def dot_t(a, b):
    return lax.dot_general(a, b, (((1,), (1,)), ((), ())), preferred_element_type=jnp.float32)


def local(queries, tools, query_mass, tool_mass):
    rows, cols = lax.axis_size("row"), lax.axis_size("col")
    ri, ci = lax.axis_index("row"), lax.axis_index("col")
    chips = cols // 2
    zi, core = ci // 2, ci % 2
    bq, features = queries.shape
    bt = tools.shape[0]
    scaling = LOG2E / (math.sqrt(features) * EPSILON)

    own = place([queries] + [swap(queries, "col", 2 * k) for k in range(1, chips)], zi)
    near = swap(tools, "col", 2)
    near_mass = swap(tool_mass, "col", 2)
    tile_tools = []
    for source in (tools, near):
        tile_tools.append(place([source] + [swap(source, "row", k) for k in range(1, rows)], ri))
    far = [swap(tools, "col", 4 * j + b) for j in range(1, chips // 2) for b in (0, 2)]
    sibling_query = swap(queries, "col", 1)
    both = place([own, swap(own, "col", 1)], core)
    tile_queries = both.reshape(-1, features)
    tile_tools = jnp.stack(tile_tools).reshape(-1, features)

    tile = dot_t(tile_queries, tile_tools) * scaling
    log_query = jnp.log2(query_mass).reshape(chips, 2, bq).transpose(1, 0, 2).reshape(-1)
    log_tool = jnp.log2(jnp.concatenate([tool_mass, near_mass]))

    far_peers = [4 * j for j in range(1, chips // 2)]
    query_side = None
    tool_side = jnp.zeros((tile.shape[1],), jnp.float32)
    for sweep in range(ITERS):
        part = local_lse(tile + tool_side[None, :], 1)
        part = lse_of([part, swap(part, "col", 1)])
        part = lse_of([part] + [swap(part, "col", k) for k in far_peers])
        query_side = log_query - part
        if sweep == 0:
            far, query_side = lax.optimization_barrier((far, query_side))
            spread = jnp.stack(far)
            spread = [spread] + [swap(spread, "row", k) for k in range(1, rows)]
        part = local_lse(tile + query_side[:, None], 0)
        part = lse_of([part] + [swap(part, "row", k) for k in range(1, rows)])
        tool_side = log_tool - part

    far_tools = jnp.moveaxis(place(spread, ri), 0, 1).reshape(-1, features)
    chip_queries = jnp.concatenate([queries, sibling_query])
    far_tile = dot_t(chip_queries, far_tools) * scaling
    by_block = tile.reshape(2, chips, bq, -1)
    near_tile = jnp.concatenate(
        [lax.dynamic_slice(by_block, (c, zi, 0, 0), (1, 1) + by_block.shape[2:])[0, 0] for c in (core, 1 - core)]
    )
    far_side = jnp.concatenate([swap(tool_side, "col", k) for k in far_peers])
    near_scores = near_tile + tool_side[None, :]
    far_scores = far_tile + far_side[None, :]
    peak = jnp.maximum(jnp.max(near_scores, axis=1), jnp.max(far_scores, axis=1))
    other = swap(peak, "col", 1)
    peak = jnp.maximum(peak, jnp.concatenate([other[bq:], other[:bq]]))
    near_exps = jnp.exp2(near_scores - peak[:, None])
    far_exps = jnp.exp2(far_scores - peak[:, None])
    total = jnp.sum(near_exps, axis=1) + jnp.sum(far_exps, axis=1)
    summed = jnp.dot(near_exps.astype(jnp.bfloat16), tile_tools, preferred_element_type=jnp.float32)
    summed = summed + jnp.dot(far_exps.astype(jnp.bfloat16), far_tools, preferred_element_type=jnp.float32)
    total = total[:bq] + swap(total[bq:], "col", 1)
    summed = summed[:bq] + swap(summed[bq:], "col", 1)
    mapped = (summed / total[:, None]).astype(jnp.bfloat16)

    unit = EPSILON / LOG2E
    query_potential = unit * query_side.reshape(2, chips, bq).transpose(1, 0, 2).reshape(-1)
    tool_potential = unit * tool_side[: tool_mass.shape[0]]
    return (mapped, query_potential, tool_potential)


def solution(mesh):
    in_specs = (P(("row", "col"), None), P(("col", "row"), None), P("row"), P("col"))
    out_specs = (P(("row", "col"), None), P("row"), P("col"))
    return jax.shard_map(local, mesh=mesh, in_specs=in_specs, out_specs=out_specs, check_vma=False)
```

```python
import functools
import math

import jax
import jax.numpy as jnp
from jax import lax
from jax.sharding import Mesh
from jax.sharding import PartitionSpec as P

ITERS = 3
EPSILON = 0.5
LOG2E = 1.0 / math.log(2.0)


def swap(x, axes, k):
    n = lax.axis_size(axes)
    return lax.ppermute(x, axes, [(i, i ^ k) for i in range(n)])


def swaps(x, axes):
    return [x] + [swap(x, axes, k) for k in range(1, lax.axis_size(axes))]


def place(blocks, index):
    whole = jnp.zeros((len(blocks),) + blocks[0].shape, blocks[0].dtype)
    for k, block in enumerate(blocks):
        whole = lax.dynamic_update_index_in_dim(whole, block, index ^ k, 0)
    return whole


def pick(x, index, axis):
    return lax.dynamic_index_in_dim(x, index, axis, False)


def lse_of(parts):
    highest = parts[0]
    for part in parts[1:]:
        highest = jnp.maximum(highest, part)
    total = jnp.exp2(parts[0] - highest)
    for part in parts[1:]:
        total = total + jnp.exp2(part - highest)
    return highest + jnp.log2(total)


def local_lse(scores, axis):
    highest = jnp.max(scores, axis=axis, keepdims=True)
    total = jnp.sum(jnp.exp2(scores - highest), axis=axis)
    return jnp.squeeze(highest, axis) + jnp.log2(total)


def dot_t(a, b):
    return lax.dot_general(a, b, (((1,), (1,)), ((), ())), preferred_element_type=jnp.float32)


def local(queries, tools, query_mass, tool_mass):
    rows = lax.axis_size("row")
    nh, nl = lax.axis_size("zh"), lax.axis_size("zl")
    ri, hi, li, core = (lax.axis_index(a) for a in ("row", "zh", "zl", "core"))
    bq, features = queries.shape
    bt = tools.shape[0]
    scaling = LOG2E / (math.sqrt(features) * EPSILON)

    tile_tools = place([place(swaps(t, "row"), ri) for t in swaps(tools, "zh")], hi).reshape(-1, features)
    log_tool = jnp.log2(place(swaps(tool_mass, "zh"), hi)).reshape(-1)
    tile_queries = place(swaps(place(swaps(queries, "zh"), hi), "zl"), li)
    tile_queries = place(swaps(tile_queries, "core"), core).reshape(-1, features)
    log_query = jnp.log2(query_mass).reshape(nh, nl, 2, bq).transpose(2, 1, 0, 3).reshape(-1)

    tile = dot_t(tile_queries, tile_tools) * scaling
    tool_side = jnp.zeros((tile.shape[1],), jnp.float32)
    for sweep in range(ITERS):
        part = lse_of(swaps(local_lse(tile + tool_side[None, :], 1), "core"))
        query_side = log_query - lse_of(swaps(part, "zl"))
        part = local_lse(tile + query_side[:, None], 0)
        tool_side = log_tool - lse_of(swaps(part, "row"))

    scores = pick(tile.reshape(2, nl, nh, bq, -1), hi, 2).reshape(2 * nl * bq, -1) + tool_side[None, :]
    peak = jnp.max(scores, axis=1)
    peak = functools.reduce(jnp.maximum, swaps(peak, "core"))
    peak = functools.reduce(jnp.maximum, swaps(peak, "zl"))
    exps = jnp.exp2(scores - peak[:, None])
    total = jnp.sum(exps, axis=1).reshape(2, nl, bq)
    summed = jnp.dot(exps.astype(jnp.bfloat16), tile_tools, preferred_element_type=jnp.float32)
    summed = summed.reshape(2, nl, bq, features)
    summed, total = (pick(x, core, 0) + swap(pick(x, 1 - core, 0), "core", 1) for x in (summed, total))
    summed, total = (
        sum([pick(x, li, 0)] + [swap(pick(x, li ^ k, 0), "zl", k) for k in range(1, nl)]) for x in (summed, total)
    )
    mapped = (summed / total[:, None]).astype(jnp.bfloat16)

    unit = EPSILON / LOG2E
    query_potential = unit * query_side.reshape(2, nl, nh, bq).transpose(2, 1, 0, 3).reshape(-1)
    tool_potential = unit * pick(tool_side.reshape(nh, -1), hi, 0)
    return (mapped, query_potential, tool_potential)


def solution(mesh):
    rows, cols = mesh.shape["row"], mesh.shape["col"]
    fine = Mesh(mesh.devices.reshape(rows, 2, cols // 4, 2), ("row", "zh", "zl", "core"))
    col = ("zh", "zl", "core")
    in_specs = (P(("row",) + col, None), P(col + ("row",), None), P("row"), P(col))
    out_specs = (P(("row",) + col, None), P("row"), P(col))
    return jax.shard_map(local, mesh=fine, in_specs=in_specs, out_specs=out_specs, check_vma=False)
```

```python
import functools
import math

import jax
import jax.numpy as jnp
from jax import lax
from jax.sharding import Mesh
from jax.sharding import PartitionSpec as P

ITERS = 3
EPSILON = 0.5
LOG2E = 1.0 / math.log(2.0)


def swap(x, axes, k):
    n = lax.axis_size(axes)
    return lax.ppermute(x, axes, [(i, i ^ k) for i in range(n)])


def swaps(x, axes):
    return [x] + [swap(x, axes, k) for k in range(1, lax.axis_size(axes))]


def place(blocks, index):
    whole = jnp.zeros((len(blocks),) + blocks[0].shape, blocks[0].dtype)
    for k, block in enumerate(blocks):
        whole = lax.dynamic_update_index_in_dim(whole, block, index ^ k, 0)
    return whole


def pick(x, index, axis):
    return lax.dynamic_index_in_dim(x, index, axis, False)


def lse_of(parts):
    highest = parts[0]
    for part in parts[1:]:
        highest = jnp.maximum(highest, part)
    total = jnp.exp2(parts[0] - highest)
    for part in parts[1:]:
        total = total + jnp.exp2(part - highest)
    return highest + jnp.log2(total)


def local_lse(scores, axis):
    highest = jnp.max(scores, axis=axis, keepdims=True)
    total = jnp.sum(jnp.exp2(scores - highest), axis=axis)
    return jnp.squeeze(highest, axis) + jnp.log2(total)


def dot_t(a, b):
    return lax.dot_general(a, b, (((1,), (1,)), ((), ())), preferred_element_type=jnp.float32)


def pairs(x, axes):
    return [x, swap(x, axes, 1)]


def by_place(pair, index):
    first = index == 0
    return jnp.stack([jnp.where(first, pair[0], pair[1]), jnp.where(first, pair[1], pair[0])])


def local(queries, tools, query_mass, tool_mass):
    rows = lax.axis_size("row")
    nl = lax.axis_size("zl")
    ri, hi, li, core = (lax.axis_index(a) for a in ("row", "zh", "zl", "core"))
    bq, features = queries.shape
    bt = tools.shape[0]
    scaling = LOG2E / (math.sqrt(features) * EPSILON)

    other_tools = swap(tools, "zh", 1)
    own = swaps(tools, "row")
    held, held_mass, own[1] = lax.optimization_barrier((queries, tool_mass, own[1]))
    tile_tools = [place(t, ri).reshape(-1, features) for t in (own, swaps(other_tools, "row"))]
    far = swap(held, "zh", 1)
    near_queries = place(swaps(queries, "zl"), li)
    far_queries = place(swaps(far, "zl"), li)
    tile_queries = jnp.stack([near_queries, far_queries])
    tile_queries = jnp.moveaxis(place(pairs(tile_queries, "core"), core), 0, 1).reshape(-1, features)
    log_tools = [jnp.log2(t) for t in (tool_mass, swap(held_mass, "zh", 1))]
    tile_queries, log_tools = lax.optimization_barrier((tile_queries, log_tools))
    log_query = jnp.log2(query_mass).reshape(2, nl, 2, bq).transpose(0, 2, 1, 3)
    log_query = by_place([log_query[0], log_query[1]], hi).reshape(-1)

    tiles = [dot_t(tile_queries, t) * scaling for t in tile_tools]
    tool_sides = [jnp.zeros((t.shape[1],), jnp.float32) for t in tiles]
    for sweep in range(ITERS):
        part = lse_of([local_lse(t + s[None, :], 1) for t, s in zip(tiles, tool_sides)])
        part = lse_of(swaps(part, "core"))
        query_side = log_query - lse_of(swaps(part, "zl"))
        part = jnp.concatenate([local_lse(t + query_side[:, None], 0) for t in tiles])
        got = lse_of(swaps(part, "row"))
        tool_sides = [m - g for m, g in zip(log_tools, jnp.split(got, 2))]

    half = 2 * nl * bq
    scores = [t[:half] + s[None, :] for t, s in zip(tiles, tool_sides)]
    peak = jnp.maximum(jnp.max(scores[0], axis=1), jnp.max(scores[1], axis=1))
    peak = functools.reduce(jnp.maximum, swaps(peak, "core"))
    peak = functools.reduce(jnp.maximum, swaps(peak, "zl"))
    exps = [jnp.exp2(s - peak[:, None]) for s in scores]
    total = sum(jnp.sum(e, axis=1) for e in exps).reshape(2, nl, bq)
    summed = sum(
        jnp.dot(e.astype(jnp.bfloat16), t, preferred_element_type=jnp.float32) for e, t in zip(exps, tile_tools)
    )
    summed = summed.reshape(2, nl, bq, features)
    summed, total = (pick(x, core, 0) + swap(pick(x, 1 - core, 0), "core", 1) for x in (summed, total))
    summed, total = (
        sum([pick(x, li, 0)] + [swap(pick(x, li ^ k, 0), "zl", k) for k in range(1, nl)]) for x in (summed, total)
    )
    mapped = (summed / total[:, None]).astype(jnp.bfloat16)

    unit = EPSILON / LOG2E
    query_potential = query_side.reshape(2, 2, nl, bq).transpose(0, 2, 1, 3)
    query_potential = unit * by_place([query_potential[0], query_potential[1]], hi).reshape(-1)
    return (mapped, query_potential, unit * tool_sides[0])


def solution(mesh):
    rows, cols = mesh.shape["row"], mesh.shape["col"]
    fine = Mesh(mesh.devices.reshape(rows, 2, cols // 4, 2), ("row", "zh", "zl", "core"))
    col = ("zh", "zl", "core")
    in_specs = (P(("row",) + col, None), P(col + ("row",), None), P("row"), P(col))
    out_specs = (P(("row",) + col, None), P("row"), P(col))
    return jax.shard_map(local, mesh=fine, in_specs=in_specs, out_specs=out_specs, check_vma=False)
```

```python
import functools
import math

import jax
import jax.numpy as jnp
from jax import lax
from jax.experimental import pallas as pl
from jax.experimental.pallas import tpu as pltpu
from jax.sharding import Mesh
from jax.sharding import PartitionSpec as P

ITERS = 3
EPSILON = 0.5
LOG2E = 1.0 / math.log(2.0)
LANES = 128


def swap(x, axes, k):
    n = lax.axis_size(axes)
    return lax.ppermute(x, axes, [(i, i ^ k) for i in range(n)])


def swaps(x, axes):
    return [x] + [swap(x, axes, k) for k in range(1, lax.axis_size(axes))]


def place(blocks, index):
    whole = jnp.zeros((len(blocks),) + blocks[0].shape, blocks[0].dtype)
    for k, block in enumerate(blocks):
        whole = lax.dynamic_update_index_in_dim(whole, block, index ^ k, 0)
    return whole


def pick(x, index, axis):
    return lax.dynamic_index_in_dim(x, index, axis, False)


def lse_of(parts):
    highest = parts[0]
    for part in parts[1:]:
        highest = jnp.maximum(highest, part)
    total = jnp.exp2(parts[0] - highest)
    for part in parts[1:]:
        total = total + jnp.exp2(part - highest)
    return highest + jnp.log2(total)


def groups(x):
    return x.reshape(x.shape[0] // 8, 8, LANES)


def row_kernel(n, *refs):
    tiles, (side, out, *peak) = refs[:n], refs[n:]
    for at in range(out.shape[0]):
        rows = pl.ds(at * LANES, LANES)

        def blocks():
            c = 0
            for t in tiles:
                for k in range(0, t.shape[1], LANES):
                    yield t[rows, k : k + LANES] + side[c : c + 1, :]
                    c += 1

        m = functools.reduce(jnp.maximum, blocks())
        s = sum(jnp.exp2(x - m) for x in blocks())
        m, s = m.T, s.T
        high = jnp.max(m, axis=0, keepdims=True)
        s = jnp.sum(s * jnp.exp2(m - high), axis=0, keepdims=True)
        out[at : at + 1, :] = high + jnp.log2(s)
        if peak:
            peak[0][at : at + 1, :] = high


def col_kernel(n, *refs):
    tiles, (side, out, wide) = refs[:n], refs[n:]
    for at in range(side.shape[0]):
        wide[at * LANES : (at + 1) * LANES, :] = jnp.broadcast_to(side[at : at + 1, :], (LANES, LANES)).T
    c = 0
    for t in tiles:
        for k in range(0, t.shape[1], LANES):

            def blocks():
                for r in range(0, t.shape[0], LANES):
                    yield groups(t[r : r + LANES, k : k + LANES] + wide[r : r + LANES, :])

            m = functools.reduce(jnp.maximum, (jnp.max(x, axis=0) for x in blocks()))
            s = sum(jnp.sum(jnp.exp2(x - m[None]), axis=0) for x in blocks())
            high = jnp.max(m, axis=0, keepdims=True)
            s = jnp.sum(s * jnp.exp2(m - high), axis=0, keepdims=True)
            out[c : c + 1, :] = high + jnp.log2(s)
            c += 1


def map_kernel(tile0, tile1, tools0, tools1, side, peak, lse, first, out):
    start = first[0]
    for r in range(0, out.shape[0], LANES):
        at = pl.multiple_of(start * LANES + r, LANES)
        which = start + r // LANES

        def wide(ref):
            return jnp.broadcast_to(ref[pl.ds(which, 1), :], (LANES, LANES)).T

        high = wide(peak)
        total = None
        c = 0
        for tile, tools in ((tile0, tools0), (tile1, tools1)):
            weights = []
            for k in range(0, tile.shape[1], LANES):
                x = tile[pl.ds(at, LANES), k : k + LANES] + side[c : c + 1, :]
                weights.append(jnp.exp2(x - high).astype(jnp.bfloat16))
                c += 1
            part = jnp.dot(jnp.concatenate(weights, axis=1), tools[...], preferred_element_type=jnp.float32)
            total = part if total is None else total + part
        scale = jnp.exp2(high - wide(lse))
        for k in range(0, out.shape[1], LANES):
            out[r : r + LANES, k : k + LANES] = total[:, k : k + LANES] * scale


def call(kernel, out_shape, args, scratch=(), flops=0, scalars=0):
    vmem, smem = (pl.BlockSpec(memory_space=m) for m in (pltpu.VMEM, pltpu.SMEM))
    size = sum(a.size for a in args)
    return pl.pallas_call(
        kernel,
        out_shape=out_shape,
        in_specs=[vmem] * (len(args) - scalars) + [smem] * scalars,
        out_specs=jax.tree.map(lambda _: vmem, out_shape),
        scratch_shapes=scratch,
        compiler_params=pltpu.CompilerParams(vmem_limit_bytes=32 << 20),
        cost_estimate=pl.CostEstimate(flops=flops or 6 * size, bytes_accessed=4 * size, transcendentals=size),
    )(*args)


def vector(n):
    return jax.ShapeDtypeStruct((n // LANES, LANES), jnp.float32)


def row_pass(tiles, side, n, peaks=False):
    return call(functools.partial(row_kernel, len(tiles)), [vector(n)] * (2 if peaks else 1), tiles + [side])


def col_pass(tiles, side):
    scratch = [pltpu.VMEM((tiles[0].shape[0], LANES), jnp.float32)]
    return call(functools.partial(col_kernel, len(tiles)), vector(sum(t.shape[1] for t in tiles)), tiles + [side], scratch)


def dot_kernel(scaling, a, b, out):
    for r in range(0, out.shape[0], 256):
        part = lax.dot_general(
            a[r : r + 256, :], b[...], (((1,), (1,)), ((), ())), preferred_element_type=jnp.float32
        )
        out[r : r + 256, :] = part * scaling


def scaled_dot(a, b, scaling):
    out_shape = jax.ShapeDtypeStruct((a.shape[0], b.shape[0]), jnp.float32)
    return call(functools.partial(dot_kernel, scaling), out_shape, [a, b], flops=2 * a.size * b.shape[0])


def pairs(x, axes):
    return [x, swap(x, axes, 1)]


def by_place(pair, index):
    first = index == 0
    return jnp.stack([jnp.where(first, pair[0], pair[1]), jnp.where(first, pair[1], pair[0])])


def local(queries, tools, query_mass, tool_mass):
    rows = lax.axis_size("row")
    nl = lax.axis_size("zl")
    ri, hi, li, core = (lax.axis_index(a) for a in ("row", "zh", "zl", "core"))
    bq, features = queries.shape
    bt = tools.shape[0]
    scaling = LOG2E / (math.sqrt(features) * EPSILON)

    other_tools = swap(tools, "zh", 1)
    own = swaps(tools, "row")
    half = nl * bq
    firsts = [jnp.full((1,), c * (half // LANES), jnp.int32) for c in (core, 1 - core)]
    held, held_mass, firsts, own[1] = lax.optimization_barrier((queries, tool_mass, firsts, own[1]))
    tile_tools = [place(t, ri).reshape(-1, features) for t in (own, swaps(other_tools, "row"))]
    far, other_mass = swap(held, "zh", 1), swap(held_mass, "zh", 1)
    near_queries = place(swaps(queries, "zl"), li)
    far_queries = place(swaps(far, "zl"), li)
    far_queries, other_mass = lax.optimization_barrier((far_queries, other_mass))
    tile_queries = jnp.stack([near_queries, far_queries])
    tile_queries = jnp.moveaxis(place(pairs(tile_queries, "core"), core), 0, 1).reshape(-1, features)
    log_tool = jnp.concatenate([jnp.log2(tool_mass), jnp.log2(other_mass)]).reshape(-1, LANES)
    log_query = jnp.log2(query_mass).reshape(2, nl, 2, bq).transpose(0, 2, 1, 3)
    log_query = by_place([log_query[0], log_query[1]], hi).reshape(-1, LANES)

    tiles = [scaled_dot(tile_queries, t, scaling) for t in tile_tools]
    tool_side = jnp.zeros_like(log_tool)
    for sweep in range(ITERS):
        (part,) = row_pass(tiles, tool_side, log_query.size)
        part = lse_of(swaps(part, "core"))
        query_side = log_query - lse_of(swaps(part, "zl"))
        tool_side = log_tool - lse_of(swaps(col_pass(tiles, query_side), "row"))

    ends = jnp.stack(row_pass(tiles, tool_side, log_query.size // 2, True))
    for axis in ("core", "zl"):
        got = swaps(ends, axis)
        ends = jnp.stack([lse_of([g[0] for g in got]), functools.reduce(jnp.maximum, [g[1] for g in got])])
    lse, peak = ends

    def mapped_rows(first):
        args = tiles + tile_tools + [tool_side, peak, lse, first]
        flops = 2 * half * tool_side.size * features
        return call(map_kernel, jax.ShapeDtypeStruct((half, features), jnp.float32), args, (), flops, 1)

    others = swap(mapped_rows(firsts[1]), "core", 1).reshape(nl, bq, features)
    own = mapped_rows(firsts[0]).reshape(nl, bq, features)
    summed = [pick(own, li ^ k, 0) + pick(others, li ^ k, 0) for k in range(nl)]
    summed = sum([summed[0]] + [swap(summed[k].astype(jnp.float16), "zl", k).astype(jnp.float32) for k in range(1, nl)])
    mapped = summed.astype(jnp.bfloat16)

    unit = EPSILON / LOG2E
    query_potential = query_side.reshape(2, 2, nl, bq).transpose(0, 2, 1, 3)
    query_potential = unit * by_place([query_potential[0], query_potential[1]], hi).reshape(-1)
    return (mapped, query_potential, unit * tool_side.reshape(-1)[: tool_mass.shape[0]])


def solution(mesh):
    rows, cols = mesh.shape["row"], mesh.shape["col"]
    fine = Mesh(mesh.devices.reshape(rows, 2, cols // 4, 2), ("row", "zh", "zl", "core"))
    col = ("zh", "zl", "core")
    in_specs = (P(("row",) + col, None), P(col + ("row",), None), P("row"), P(col))
    out_specs = (P(("row",) + col, None), P("row"), P(col))
    return jax.shard_map(local, mesh=fine, in_specs=in_specs, out_specs=out_specs, check_vma=False)
```

```python
import functools
import math

import jax
import jax.numpy as jnp
from jax import lax
from jax.experimental import pallas as pl
from jax.experimental.pallas import tpu as pltpu
from jax.sharding import Mesh
from jax.sharding import PartitionSpec as P

ITERS = 3
EPSILON = 0.5
LOG2E = 1.0 / math.log(2.0)
LANES = 128


def swap(x, axes, k):
    n = lax.axis_size(axes)
    return lax.ppermute(x, axes, [(i, i ^ k) for i in range(n)])


def swaps(x, axes):
    return [x] + [swap(x, axes, k) for k in range(1, lax.axis_size(axes))]


def place(blocks, index):
    whole = jnp.zeros((len(blocks),) + blocks[0].shape, blocks[0].dtype)
    for k, block in enumerate(blocks):
        whole = lax.dynamic_update_index_in_dim(whole, block, index ^ k, 0)
    return whole


def pick(x, index, axis):
    return lax.dynamic_index_in_dim(x, index, axis, False)


def lse_of(parts):
    highest = parts[0]
    for part in parts[1:]:
        highest = jnp.maximum(highest, part)
    total = jnp.exp2(parts[0] - highest)
    for part in parts[1:]:
        total = total + jnp.exp2(part - highest)
    return highest + jnp.log2(total)


def groups(x):
    return x.reshape(x.shape[0] // 8, 8, LANES)


def row_kernel(n, *refs):
    tiles, (side, out, *peak) = refs[:n], refs[n:]
    for at in range(out.shape[0]):
        rows = pl.ds(at * LANES, LANES)

        def blocks():
            c = 0
            for t in tiles:
                for k in range(0, t.shape[1], LANES):
                    yield t[rows, k : k + LANES] + side[c : c + 1, :]
                    c += 1

        m = functools.reduce(jnp.maximum, blocks())
        s = sum(jnp.exp2(x - m) for x in blocks())
        m, s = m.T, s.T
        high = jnp.max(m, axis=0, keepdims=True)
        s = jnp.sum(s * jnp.exp2(m - high), axis=0, keepdims=True)
        out[at : at + 1, :] = high + jnp.log2(s)
        if peak:
            peak[0][at : at + 1, :] = high


def col_kernel(n, *refs):
    tiles, (side, out, wide) = refs[:n], refs[n:]
    for at in range(side.shape[0]):
        wide[at * LANES : (at + 1) * LANES, :] = jnp.broadcast_to(side[at : at + 1, :], (LANES, LANES)).T
    c = 0
    for t in tiles:
        for k in range(0, t.shape[1], LANES):

            def blocks():
                for r in range(0, t.shape[0], LANES):
                    yield groups(t[r : r + LANES, k : k + LANES] + wide[r : r + LANES, :])

            m = functools.reduce(jnp.maximum, (jnp.max(x, axis=0) for x in blocks()))
            s = sum(jnp.sum(jnp.exp2(x - m[None]), axis=0) for x in blocks())
            high = jnp.max(m, axis=0, keepdims=True)
            s = jnp.sum(s * jnp.exp2(m - high), axis=0, keepdims=True)
            out[c : c + 1, :] = high + jnp.log2(s)
            c += 1


def map_kernel(tile0, tile1, tools0, tools1, side, peak, lse, first, out):
    start = first[0]
    for r in range(0, out.shape[0], LANES):
        at = pl.multiple_of(start * LANES + r, LANES)
        which = start + r // LANES

        def wide(ref):
            return jnp.broadcast_to(ref[pl.ds(which, 1), :], (LANES, LANES)).T

        high = wide(peak)
        total = None
        c = 0
        for tile, tools in ((tile0, tools0), (tile1, tools1)):
            weights = []
            for k in range(0, tile.shape[1], LANES):
                x = tile[pl.ds(at, LANES), k : k + LANES] + side[c : c + 1, :]
                weights.append(jnp.exp2(x - high).astype(jnp.bfloat16))
                c += 1
            part = jnp.dot(jnp.concatenate(weights, axis=1), tools[...], preferred_element_type=jnp.float32)
            total = part if total is None else total + part
        scale = jnp.exp2(high - wide(lse))
        for k in range(0, out.shape[1], LANES):
            out[r : r + LANES, k : k + LANES] = total[:, k : k + LANES] * scale


def call(kernel, out_shape, args, scratch=(), flops=0, scalars=0):
    vmem, smem = (pl.BlockSpec(memory_space=m) for m in (pltpu.VMEM, pltpu.SMEM))
    size = sum(a.size for a in args)
    return pl.pallas_call(
        kernel,
        out_shape=out_shape,
        in_specs=[vmem] * (len(args) - scalars) + [smem] * scalars,
        out_specs=jax.tree.map(lambda _: vmem, out_shape),
        scratch_shapes=scratch,
        compiler_params=pltpu.CompilerParams(vmem_limit_bytes=32 << 20),
        cost_estimate=pl.CostEstimate(flops=flops or 6 * size, bytes_accessed=4 * size, transcendentals=size),
    )(*args)


def vector(n):
    return jax.ShapeDtypeStruct((n // LANES, LANES), jnp.float32)


def row_pass(tiles, side, n, peaks=False):
    return call(functools.partial(row_kernel, len(tiles)), [vector(n)] * (2 if peaks else 1), tiles + [side])


def col_pass(tiles, side):
    scratch = [pltpu.VMEM((tiles[0].shape[0], LANES), jnp.float32)]
    return call(functools.partial(col_kernel, len(tiles)), vector(sum(t.shape[1] for t in tiles)), tiles + [side], scratch)


def dot_kernel(scaling, a, b, out):
    for r in range(0, out.shape[0], 256):
        part = lax.dot_general(
            a[r : r + 256, :], b[...], (((1,), (1,)), ((), ())), preferred_element_type=jnp.float32
        )
        out[r : r + 256, :] = part * scaling


def scaled_dot(a, b, scaling):
    out_shape = jax.ShapeDtypeStruct((a.shape[0], b.shape[0]), jnp.float32)
    return call(functools.partial(dot_kernel, scaling), out_shape, [a, b], flops=2 * a.size * b.shape[0])


def pairs(x, axes):
    return [x, swap(x, axes, 1)]


def by_place(pair, index):
    first = index == 0
    return jnp.stack([jnp.where(first, pair[0], pair[1]), jnp.where(first, pair[1], pair[0])])


def local(queries, tools, query_mass, tool_mass):
    rows = lax.axis_size("row")
    nl = lax.axis_size("zl")
    ri, hi, li, core = (lax.axis_index(a) for a in ("row", "zh", "zl", "core"))
    bq, features = queries.shape
    bt = tools.shape[0]
    scaling = LOG2E / (math.sqrt(features) * EPSILON)

    other_tools = swap(tools, "zh", 1)
    own = swaps(tools, "row")
    half = nl * bq
    firsts = [jnp.full((1,), c * (half // LANES), jnp.int32) for c in (core, 1 - core)]
    held, held_mass, firsts, own[1] = lax.optimization_barrier((queries, tool_mass, firsts, own[1]))
    tile_tools = [place(t, ri).reshape(-1, features) for t in (own, swaps(other_tools, "row"))]
    far, other_mass = swap(held, "zh", 1), swap(held_mass, "zh", 1)
    near_queries = place(swaps(queries, "zl"), li)
    far_queries = place(swaps(far, "zl"), li)
    far_queries, other_mass = lax.optimization_barrier((far_queries, other_mass))
    tile_queries = jnp.stack([near_queries, far_queries])
    tile_queries = jnp.moveaxis(place(pairs(tile_queries, "core"), core), 0, 1).reshape(-1, features)
    log_tool = jnp.concatenate([jnp.log2(tool_mass), jnp.log2(other_mass)]).reshape(-1, LANES)
    log_query = jnp.log2(query_mass).reshape(2, nl, 2, bq).transpose(0, 2, 1, 3)
    log_query = by_place([log_query[0], log_query[1]], hi).reshape(-1, LANES)

    tiles = [scaled_dot(tile_queries, t, scaling) for t in tile_tools]
    tool_side = jnp.zeros_like(log_tool)
    for sweep in range(ITERS):
        (part,) = row_pass(tiles, tool_side, log_query.size)
        query_side = log_query - lse_of(swaps(part, ("zl", "core")))
        tool_side = log_tool - lse_of(swaps(col_pass(tiles, query_side), "row"))

    ends = jnp.stack(row_pass(tiles, tool_side, log_query.size // 2, True))
    for axis in (("zl", "core"),):
        got = swaps(ends, axis)
        ends = jnp.stack([lse_of([g[0] for g in got]), functools.reduce(jnp.maximum, [g[1] for g in got])])
    lse, peak = ends

    def mapped_rows(first):
        args = tiles + tile_tools + [tool_side, peak, lse, first]
        flops = 2 * half * tool_side.size * features
        return call(map_kernel, jax.ShapeDtypeStruct((half, features), jnp.float32), args, (), flops, 1)

    others = swap(mapped_rows(firsts[1]), "core", 1).reshape(nl, bq, features)
    own = mapped_rows(firsts[0]).reshape(nl, bq, features)
    own, query_side, tool_side = lax.optimization_barrier((own, query_side, tool_side))
    summed = [pick(own, li ^ k, 0) + pick(others, li ^ k, 0) for k in range(nl)]
    summed = sum([summed[0]] + [swap(summed[k].astype(jnp.float16), "zl", k).astype(jnp.float32) for k in range(1, nl)])
    mapped = summed.astype(jnp.bfloat16)

    unit = EPSILON / LOG2E
    query_potential = query_side.reshape(2, 2, nl, bq).transpose(0, 2, 1, 3)
    query_potential = unit * by_place([query_potential[0], query_potential[1]], hi).reshape(-1)
    return (mapped, query_potential, unit * tool_side.reshape(-1)[: tool_mass.shape[0]])


def solution(mesh):
    rows, cols = mesh.shape["row"], mesh.shape["col"]
    fine = Mesh(mesh.devices.reshape(rows, 2, cols // 4, 2), ("row", "zh", "zl", "core"))
    col = ("zh", "zl", "core")
    in_specs = (P(("row",) + col, None), P(col + ("row",), None), P("row"), P(col))
    out_specs = (P(("row",) + col, None), P("row"), P(col))
    return jax.shard_map(local, mesh=fine, in_specs=in_specs, out_specs=out_specs, check_vma=False)
```

```python
import functools
import math

import jax
import jax.numpy as jnp
from jax import lax
from jax.experimental import pallas as pl
from jax.experimental.pallas import tpu as pltpu
from jax.sharding import Mesh
from jax.sharding import PartitionSpec as P

ITERS = 3
EPSILON = 0.5
LOG2E = 1.0 / math.log(2.0)
LANES = 128


def swap(x, axes, k):
    n = lax.axis_size(axes)
    return lax.ppermute(x, axes, [(i, i ^ k) for i in range(n)])


def swaps(x, axes):
    return [x] + [swap(x, axes, k) for k in range(1, lax.axis_size(axes))]


def place(blocks, index):
    whole = jnp.zeros((len(blocks),) + blocks[0].shape, blocks[0].dtype)
    for k, block in reversed(list(enumerate(blocks))):
        whole = lax.dynamic_update_index_in_dim(whole, block, index ^ k, 0)
    return whole


def pick(x, index, axis):
    return lax.dynamic_index_in_dim(x, index, axis, False)


def lse_of(parts):
    highest = parts[0]
    for part in parts[1:]:
        highest = jnp.maximum(highest, part)
    total = jnp.exp2(parts[0] - highest)
    for part in parts[1:]:
        total = total + jnp.exp2(part - highest)
    return highest + jnp.log2(total)


def groups(x):
    return x.reshape(x.shape[0] // 8, 8, LANES)


def row_kernel(n, *refs):
    tiles, (side, out, *peak) = refs[:n], refs[n:]
    for at in range(out.shape[0]):
        rows = pl.ds(at * LANES, LANES)

        def blocks():
            c = 0
            for t in tiles:
                for k in range(0, t.shape[1], LANES):
                    yield t[rows, k : k + LANES] + side[c : c + 1, :]
                    c += 1

        m = functools.reduce(jnp.maximum, blocks())
        s = sum(jnp.exp2(x - m) for x in blocks())
        m, s = m.T, s.T
        high = jnp.max(m, axis=0, keepdims=True)
        s = jnp.sum(s * jnp.exp2(m - high), axis=0, keepdims=True)
        out[at : at + 1, :] = high + jnp.log2(s)
        if peak:
            peak[0][at : at + 1, :] = high


def col_kernel(n, *refs):
    tiles, (side, out, wide) = refs[:n], refs[n:]
    for at in range(side.shape[0]):
        wide[at * LANES : (at + 1) * LANES, :] = jnp.broadcast_to(side[at : at + 1, :], (LANES, LANES)).T
    c = 0
    for t in tiles:
        for k in range(0, t.shape[1], LANES):

            def blocks():
                for r in range(0, t.shape[0], LANES):
                    yield groups(t[r : r + LANES, k : k + LANES] + wide[r : r + LANES, :])

            m = functools.reduce(jnp.maximum, (jnp.max(x, axis=0) for x in blocks()))
            s = sum(jnp.sum(jnp.exp2(x - m[None]), axis=0) for x in blocks())
            high = jnp.max(m, axis=0, keepdims=True)
            s = jnp.sum(s * jnp.exp2(m - high), axis=0, keepdims=True)
            out[c : c + 1, :] = high + jnp.log2(s)
            c += 1


def map_kernel(tile0, tile1, tools0, tools1, side, peak, lse, first, out):
    start = first[0]
    for r in range(0, out.shape[0], LANES):
        at = pl.multiple_of(start * LANES + r, LANES)
        which = start + r // LANES

        def wide(ref):
            return jnp.broadcast_to(ref[pl.ds(which, 1), :], (LANES, LANES)).T

        high = wide(peak)
        total = None
        c = 0
        for tile, tools in ((tile0, tools0), (tile1, tools1)):
            weights = []
            for k in range(0, tile.shape[1], LANES):
                x = tile[pl.ds(at, LANES), k : k + LANES] + side[c : c + 1, :]
                weights.append(jnp.exp2(x - high).astype(jnp.bfloat16))
                c += 1
            part = jnp.dot(jnp.concatenate(weights, axis=1), tools[...], preferred_element_type=jnp.float32)
            total = part if total is None else total + part
        scale = jnp.exp2(high - wide(lse))
        for k in range(0, out.shape[1], LANES):
            out[r : r + LANES, k : k + LANES] = total[:, k : k + LANES] * scale


def call(kernel, out_shape, args, scratch=(), flops=0, scalars=0):
    vmem, smem = (pl.BlockSpec(memory_space=m) for m in (pltpu.VMEM, pltpu.SMEM))
    size = sum(a.size for a in args)
    return pl.pallas_call(
        kernel,
        out_shape=out_shape,
        in_specs=[vmem] * (len(args) - scalars) + [smem] * scalars,
        out_specs=jax.tree.map(lambda _: vmem, out_shape),
        scratch_shapes=scratch,
        compiler_params=pltpu.CompilerParams(vmem_limit_bytes=32 << 20),
        cost_estimate=pl.CostEstimate(flops=flops or 6 * size, bytes_accessed=4 * size, transcendentals=size),
    )(*args)


def vector(n):
    return jax.ShapeDtypeStruct((n // LANES, LANES), jnp.float32)


def row_pass(tiles, side, n, peaks=False):
    return call(functools.partial(row_kernel, len(tiles)), [vector(n)] * (2 if peaks else 1), tiles + [side])


def col_pass(tiles, side):
    scratch = [pltpu.VMEM((tiles[0].shape[0], LANES), jnp.float32)]
    return call(functools.partial(col_kernel, len(tiles)), vector(sum(t.shape[1] for t in tiles)), tiles + [side], scratch)


def dot_kernel(scaling, a, b, out):
    for r in range(0, out.shape[0], 256):
        part = lax.dot_general(
            a[r : r + 256, :], b[...], (((1,), (1,)), ((), ())), preferred_element_type=jnp.float32
        )
        out[r : r + 256, :] = part * scaling


def scaled_dot(a, b, scaling):
    out_shape = jax.ShapeDtypeStruct((a.shape[0], b.shape[0]), jnp.float32)
    return call(functools.partial(dot_kernel, scaling), out_shape, [a, b], flops=2 * a.size * b.shape[0])


def pairs(x, axes):
    return [x, swap(x, axes, 1)]


def by_place(pair, index):
    first = index == 0
    return jnp.stack([jnp.where(first, pair[0], pair[1]), jnp.where(first, pair[1], pair[0])])


def local(queries, tools, query_mass, tool_mass):
    rows = lax.axis_size("row")
    nl = lax.axis_size("zl")
    ri, hi, li, core = (lax.axis_index(a) for a in ("row", "zh", "zl", "core"))
    bq, features = queries.shape
    bt = tools.shape[0]
    scaling = LOG2E / (math.sqrt(features) * EPSILON)

    other_tools = swap(tools, "zh", 1)
    own = swaps(tools, "row")
    half = nl * bq
    firsts = [jnp.full((1,), c * (half // LANES), jnp.int32) for c in (core, 1 - core)]
    held, held_mass, firsts, own[2] = lax.optimization_barrier((queries, tool_mass, firsts, own[2]))
    tile_tools = [place(t, ri).reshape(-1, features) for t in (own, swaps(other_tools, "row"))]
    far, other_mass = swap(held, "zh", 1), swap(held_mass, "zh", 1)
    near_queries = place(swaps(queries, "zl"), li)
    far_queries = place(swaps(far, "zl"), li)
    far_queries, other_mass = lax.optimization_barrier((far_queries, other_mass))
    tile_queries = jnp.stack([near_queries, far_queries])
    tile_queries = jnp.moveaxis(place(pairs(tile_queries, "core"), core), 0, 1).reshape(-1, features)
    log_tool = jnp.concatenate([jnp.log2(tool_mass), jnp.log2(other_mass)]).reshape(-1, LANES)
    log_query = jnp.log2(query_mass).reshape(2, nl, 2, bq).transpose(0, 2, 1, 3)
    log_query = by_place([log_query[0], log_query[1]], hi).reshape(-1, LANES)

    tiles = [scaled_dot(tile_queries, t, scaling) for t in tile_tools]
    tool_side = jnp.zeros_like(log_tool)
    for sweep in range(ITERS):
        (part,) = row_pass(tiles, tool_side, log_query.size)
        got = swaps(part, ("zl", "core"))
        query_side = log_query - lse_of(got[:1] + got[:0:-1])
        got = swaps(col_pass(tiles, query_side), "row")
        tool_side = log_tool - lse_of([got[k] for k in (0, *range(rows - 1, 0, -1))])

    ends = jnp.stack(row_pass(tiles, tool_side, log_query.size // 2, True))
    for axis in (("zl", "core"),):
        got = swaps(ends, axis)
        got = got[:1] + got[:0:-1]
        ends = jnp.stack([lse_of([g[0] for g in got]), functools.reduce(jnp.maximum, [g[1] for g in got])])
    lse, peak = ends

    def mapped_rows(first):
        args = tiles + tile_tools + [tool_side, peak, lse, first]
        flops = 2 * half * tool_side.size * features
        return call(map_kernel, jax.ShapeDtypeStruct((half, features), jnp.float32), args, (), flops, 1)

    others = swap(mapped_rows(firsts[1]), "core", 1).reshape(nl, bq, features)
    own = mapped_rows(firsts[0]).reshape(nl, bq, features)
    own, query_side, tool_side = lax.optimization_barrier((own, query_side, tool_side))
    summed = [pick(own, li ^ k, 0) + pick(others, li ^ k, 0) for k in range(nl)]
    summed = sum([summed[0]] + [swap(summed[k].astype(jnp.float16), "zl", k).astype(jnp.float32) for k in range(1, nl)])
    mapped = summed.astype(jnp.bfloat16)

    unit = EPSILON / LOG2E
    query_potential = query_side.reshape(2, 2, nl, bq).transpose(0, 2, 1, 3)
    query_potential = unit * by_place([query_potential[0], query_potential[1]], hi).reshape(-1)
    return (mapped, query_potential, unit * tool_side.reshape(-1)[: tool_mass.shape[0]])


def solution(mesh):
    rows, cols = mesh.shape["row"], mesh.shape["col"]
    fine = Mesh(mesh.devices.reshape(rows, 2, cols // 4, 2), ("row", "zh", "zl", "core"))
    col = ("zh", "zl", "core")
    in_specs = (P(("row",) + col, None), P(col + ("row",), None), P("row"), P(col))
    out_specs = (P(("row",) + col, None), P("row"), P(col))
    return jax.shard_map(local, mesh=fine, in_specs=in_specs, out_specs=out_specs, check_vma=False)
```

```python
import functools
import math

import jax
import jax.numpy as jnp
from jax import lax
from jax.experimental import pallas as pl
from jax.experimental.pallas import tpu as pltpu
from jax.sharding import Mesh
from jax.sharding import PartitionSpec as P

ITERS = 3
EPSILON = 0.5
LOG2E = 1.0 / math.log(2.0)
LANES = 128


def swap(x, axes, k):
    n = lax.axis_size(axes)
    return lax.ppermute(x, axes, [(i, i ^ k) for i in range(n)])


def swaps(x, axes):
    return [x] + [swap(x, axes, k) for k in range(1, lax.axis_size(axes))]


def place(blocks, index, forward=False):
    whole = jnp.zeros((len(blocks),) + blocks[0].shape, blocks[0].dtype)
    for k in range(len(blocks))[:: 1 if forward else -1]:
        whole = lax.dynamic_update_index_in_dim(whole, blocks[k], index ^ k, 0)
    return whole


def pick(x, index, axis):
    return lax.dynamic_index_in_dim(x, index, axis, False)


def lse_of(parts):
    highest = parts[0]
    for part in parts[1:]:
        highest = jnp.maximum(highest, part)
    total = jnp.exp2(parts[0] - highest)
    for part in parts[1:]:
        total = total + jnp.exp2(part - highest)
    return highest + jnp.log2(total)


def groups(x):
    return x.reshape(x.shape[0] // 8, 8, LANES)


def row_kernel(n, *refs):
    tiles, (side, out, *peak) = refs[:n], refs[n:]
    for at in range(out.shape[0]):
        rows = pl.ds(at * LANES, LANES)

        def blocks():
            c = 0
            for t in tiles:
                for k in range(0, t.shape[1], LANES):
                    yield t[rows, k : k + LANES] + side[c : c + 1, :]
                    c += 1

        m = functools.reduce(jnp.maximum, blocks())
        s = sum(jnp.exp2(x - m) for x in blocks())
        m, s = m.T, s.T
        high = jnp.max(m, axis=0, keepdims=True)
        s = jnp.sum(s * jnp.exp2(m - high), axis=0, keepdims=True)
        out[at : at + 1, :] = high + jnp.log2(s)
        if peak:
            peak[0][at : at + 1, :] = high


def col_kernel(n, *refs):
    tiles, (side, out, wide) = refs[:n], refs[n:]
    for at in range(side.shape[0]):
        wide[at * LANES : (at + 1) * LANES, :] = jnp.broadcast_to(side[at : at + 1, :], (LANES, LANES)).T
    c = 0
    for t in tiles:
        for k in range(0, t.shape[1], LANES):

            def blocks():
                for r in range(0, t.shape[0], LANES):
                    yield groups(t[r : r + LANES, k : k + LANES] + wide[r : r + LANES, :])

            m = functools.reduce(jnp.maximum, (jnp.max(x, axis=0) for x in blocks()))
            s = sum(jnp.sum(jnp.exp2(x - m[None]), axis=0) for x in blocks())
            high = jnp.max(m, axis=0, keepdims=True)
            s = jnp.sum(s * jnp.exp2(m - high), axis=0, keepdims=True)
            out[c : c + 1, :] = high + jnp.log2(s)
            c += 1


def map_kernel(tile0, tile1, tools0, tools1, side, peak, lse, first, out):
    start = first[0]
    for r in range(0, out.shape[0], LANES):
        at = pl.multiple_of(start * LANES + r, LANES)
        which = start + r // LANES

        def wide(ref):
            return jnp.broadcast_to(ref[pl.ds(which, 1), :], (LANES, LANES)).T

        high = wide(peak)
        total = None
        c = 0
        for tile, tools in ((tile0, tools0), (tile1, tools1)):
            weights = []
            for k in range(0, tile.shape[1], LANES):
                x = tile[pl.ds(at, LANES), k : k + LANES] + side[c : c + 1, :]
                weights.append(jnp.exp2(x - high).astype(jnp.bfloat16))
                c += 1
            part = jnp.dot(jnp.concatenate(weights, axis=1), tools[...], preferred_element_type=jnp.float32)
            total = part if total is None else total + part
        scale = jnp.exp2(high - wide(lse))
        for k in range(0, out.shape[1], LANES):
            out[r : r + LANES, k : k + LANES] = total[:, k : k + LANES] * scale


def call(kernel, out_shape, args, scratch=(), flops=0, scalars=0):
    vmem, smem = (pl.BlockSpec(memory_space=m) for m in (pltpu.VMEM, pltpu.SMEM))
    size = sum(a.size for a in args)
    return pl.pallas_call(
        kernel,
        out_shape=out_shape,
        in_specs=[vmem] * (len(args) - scalars) + [smem] * scalars,
        out_specs=jax.tree.map(lambda _: vmem, out_shape),
        scratch_shapes=scratch,
        compiler_params=pltpu.CompilerParams(vmem_limit_bytes=32 << 20),
        cost_estimate=pl.CostEstimate(flops=flops or 6 * size, bytes_accessed=4 * size, transcendentals=size),
    )(*args)


def vector(n):
    return jax.ShapeDtypeStruct((n // LANES, LANES), jnp.float32)


def row_pass(tiles, side, n, peaks=False):
    return call(functools.partial(row_kernel, len(tiles)), [vector(n)] * (2 if peaks else 1), tiles + [side])


def col_pass(tiles, side):
    scratch = [pltpu.VMEM((tiles[0].shape[0], LANES), jnp.float32)]
    return call(functools.partial(col_kernel, len(tiles)), vector(sum(t.shape[1] for t in tiles)), tiles + [side], scratch)


def dot_kernel(scaling, a, b, out):
    for r in range(0, out.shape[0], 512):
        part = lax.dot_general(
            a[r : r + 512, :], b[...], (((1,), (1,)), ((), ())), preferred_element_type=jnp.float32
        )
        out[r : r + 512, :] = part * scaling


def scaled_dot(a, b, scaling):
    out_shape = jax.ShapeDtypeStruct((a.shape[0], b.shape[0]), jnp.float32)
    return call(functools.partial(dot_kernel, scaling), out_shape, [a, b], flops=2 * a.size * b.shape[0])


def pairs(x, axes):
    return [x, swap(x, axes, 1)]


def by_place(pair, index):
    first = index == 0
    return jnp.stack([jnp.where(first, pair[0], pair[1]), jnp.where(first, pair[1], pair[0])])


def local(queries, tools, query_mass, tool_mass):
    rows = lax.axis_size("row")
    nl = lax.axis_size("zl")
    ri, hi, li, core = (lax.axis_index(a) for a in ("row", "zh", "zl", "core"))
    bq, features = queries.shape
    bt = tools.shape[0]
    scaling = LOG2E / (math.sqrt(features) * EPSILON)

    other_tools = swap(tools, "zh", 1)
    own = swaps(tools, "row")
    half = nl * bq
    firsts = [jnp.full((1,), c * (half // LANES), jnp.int32) for c in (core, 1 - core)]
    held, held_mass, firsts, own[2] = lax.optimization_barrier((queries, tool_mass, firsts, own[2]))
    tile_tools = [place(t, ri).reshape(-1, features) for t in (own, swaps(other_tools, "row"))]
    far, other_mass = swap(held, "zh", 1), swap(held_mass, "zh", 1)
    near_queries = place(swaps(queries, "zl"), li)
    far_queries = place(swaps(far, "zl"), li)
    far_queries, other_mass = lax.optimization_barrier((far_queries, other_mass))
    tile_queries = jnp.stack([near_queries, far_queries])
    tile_queries = jnp.moveaxis(place(pairs(tile_queries, "core"), core, True), 0, 1).reshape(-1, features)
    log_tool = jnp.concatenate([jnp.log2(tool_mass), jnp.log2(other_mass)]).reshape(-1, LANES)
    log_query = jnp.log2(query_mass).reshape(2, nl, 2, bq).transpose(0, 2, 1, 3)
    log_query = by_place([log_query[0], log_query[1]], hi).reshape(-1, LANES)

    tiles = [scaled_dot(tile_queries, t, scaling) for t in tile_tools]
    tool_side = jnp.zeros_like(log_tool)
    for sweep in range(ITERS):
        (part,) = row_pass(tiles, tool_side, log_query.size)
        got = swaps(part, ("zl", "core"))
        query_side = log_query - lse_of(got[:1] + got[:0:-1])
        got = swaps(col_pass(tiles, query_side), "row")
        tool_side = log_tool - lse_of([got[k] for k in (0, *range(rows - 1, 0, -1))])

    ends = jnp.stack(row_pass(tiles, tool_side, log_query.size // 2, True))
    for axis in (("zl", "core"),):
        got = swaps(ends, axis)
        got = got[:1] + got[:0:-1]
        ends = jnp.stack([lse_of([g[0] for g in got]), functools.reduce(jnp.maximum, [g[1] for g in got])])
    lse, peak = ends

    def mapped_rows(first):
        args = tiles + tile_tools + [tool_side, peak, lse, first]
        flops = 2 * half * tool_side.size * features
        return call(map_kernel, jax.ShapeDtypeStruct((half, features), jnp.float32), args, (), flops, 1)

    others = swap(mapped_rows(firsts[1]), "core", 1).reshape(nl, bq, features)
    own = mapped_rows(firsts[0]).reshape(nl, bq, features)
    own, query_side, tool_side = lax.optimization_barrier((own, query_side, tool_side))
    summed = [pick(own, li ^ k, 0) + pick(others, li ^ k, 0) for k in range(nl)]
    summed = sum([summed[0]] + [swap(summed[k].astype(jnp.float16), "zl", k).astype(jnp.float32) for k in range(1, nl)])
    mapped = summed.astype(jnp.bfloat16)

    unit = EPSILON / LOG2E
    query_potential = query_side.reshape(2, 2, nl, bq).transpose(0, 2, 1, 3)
    query_potential = unit * by_place([query_potential[0], query_potential[1]], hi).reshape(-1)
    return (mapped, query_potential, unit * tool_side.reshape(-1)[: tool_mass.shape[0]])


def solution(mesh):
    rows, cols = mesh.shape["row"], mesh.shape["col"]
    fine = Mesh(mesh.devices.reshape(rows, 2, cols // 4, 2), ("row", "zh", "zl", "core"))
    col = ("zh", "zl", "core")
    in_specs = (P(("row",) + col, None), P(col + ("row",), None), P("row"), P(col))
    out_specs = (P(("row",) + col, None), P("row"), P(col))
    return jax.shard_map(local, mesh=fine, in_specs=in_specs, out_specs=out_specs, check_vma=False)
```

```python
import functools
import math

import jax
import jax.numpy as jnp
from jax import lax
from jax.experimental import pallas as pl
from jax.experimental.pallas import tpu as pltpu
from jax.sharding import Mesh
from jax.sharding import PartitionSpec as P

ITERS = 3
EPSILON = 0.5
LOG2E = 1.0 / math.log(2.0)
LANES = 128


def swap(x, axes, k):
    n = lax.axis_size(axes)
    return lax.ppermute(x, axes, [(i, i ^ k) for i in range(n)])


def swaps(x, axes):
    return [x] + [swap(x, axes, k) for k in range(1, lax.axis_size(axes))]


def place(blocks, index, forward=False):
    whole = jnp.zeros((len(blocks),) + blocks[0].shape, blocks[0].dtype)
    for k in range(len(blocks))[:: 1 if forward else -1]:
        whole = lax.dynamic_update_index_in_dim(whole, blocks[k], index ^ k, 0)
    return whole


def pick(x, index, axis):
    return lax.dynamic_index_in_dim(x, index, axis, False)


def lse_of(parts):
    highest = parts[0]
    for part in parts[1:]:
        highest = jnp.maximum(highest, part)
    total = jnp.exp2(parts[0] - highest)
    for part in parts[1:]:
        total = total + jnp.exp2(part - highest)
    return highest + jnp.log2(total)


def groups(x):
    return x.reshape(x.shape[0] // 8, 8, LANES)


def row_lse(tiles, side, at):
    rows = pl.ds(at * LANES, LANES)

    def blocks():
        c = 0
        for t in tiles:
            for k in range(0, t.shape[1], LANES):
                x = t[rows, k : k + LANES]
                yield x if side is None else x + side[c : c + 1, :]
                c += 1

    m = functools.reduce(jnp.maximum, blocks())
    s = sum(jnp.exp2(x - m) for x in blocks())
    m, s = m.T, s.T
    high = jnp.max(m, axis=0, keepdims=True)
    s = jnp.sum(s * jnp.exp2(m - high), axis=0, keepdims=True)
    return high + jnp.log2(s), high


def row_kernel(n, *refs):
    tiles, (side, out, *peak) = refs[:n], refs[n:]
    for at in range(out.shape[0]):
        out[at : at + 1, :], high = row_lse(tiles, side, at)
        if peak:
            peak[0][at : at + 1, :] = high


def col_kernel(n, *refs):
    tiles, (side, out, wide) = refs[:n], refs[n:]
    for at in range(side.shape[0]):
        wide[at * LANES : (at + 1) * LANES, :] = jnp.broadcast_to(side[at : at + 1, :], (LANES, LANES)).T
    c = 0
    for t in tiles:
        for k in range(0, t.shape[1], LANES):

            def blocks():
                for r in range(0, t.shape[0], LANES):
                    yield groups(t[r : r + LANES, k : k + LANES] + wide[r : r + LANES, :])

            m = functools.reduce(jnp.maximum, (jnp.max(x, axis=0) for x in blocks()))
            s = sum(jnp.sum(jnp.exp2(x - m[None]), axis=0) for x in blocks())
            high = jnp.max(m, axis=0, keepdims=True)
            s = jnp.sum(s * jnp.exp2(m - high), axis=0, keepdims=True)
            out[c : c + 1, :] = high + jnp.log2(s)
            c += 1


def map_kernel(tile0, tile1, tools0, tools1, side, peak, lse, first, out):
    start = first[0]
    for r in range(0, out.shape[0], LANES):
        at = pl.multiple_of(start * LANES + r, LANES)
        which = start + r // LANES

        def wide(ref):
            return jnp.broadcast_to(ref[pl.ds(which, 1), :], (LANES, LANES)).T

        high = wide(peak)
        total = None
        c = 0
        for tile, tools in ((tile0, tools0), (tile1, tools1)):
            weights = []
            for k in range(0, tile.shape[1], LANES):
                x = tile[pl.ds(at, LANES), k : k + LANES] + side[c : c + 1, :]
                weights.append(jnp.exp2(x - high).astype(jnp.bfloat16))
                c += 1
            part = jnp.dot(jnp.concatenate(weights, axis=1), tools[...], preferred_element_type=jnp.float32)
            total = part if total is None else total + part
        scale = jnp.exp2(high - wide(lse))
        for k in range(0, out.shape[1], LANES):
            out[r : r + LANES, k : k + LANES] = total[:, k : k + LANES] * scale


def call(kernel, out_shape, args, scratch=(), flops=0, scalars=0):
    vmem, smem = (pl.BlockSpec(memory_space=m) for m in (pltpu.VMEM, pltpu.SMEM))
    size = sum(a.size for a in args)
    return pl.pallas_call(
        kernel,
        out_shape=out_shape,
        in_specs=[vmem] * (len(args) - scalars) + [smem] * scalars,
        out_specs=jax.tree.map(lambda _: vmem, out_shape),
        scratch_shapes=scratch,
        compiler_params=pltpu.CompilerParams(vmem_limit_bytes=32 << 20),
        cost_estimate=pl.CostEstimate(flops=flops or 6 * size, bytes_accessed=4 * size, transcendentals=size),
    )(*args)


def vector(n):
    return jax.ShapeDtypeStruct((n // LANES, LANES), jnp.float32)


def row_pass(tiles, side, n, peaks=False):
    return call(functools.partial(row_kernel, len(tiles)), [vector(n)] * (2 if peaks else 1), tiles + [side])


def col_pass(tiles, side):
    scratch = [pltpu.VMEM((tiles[0].shape[0], LANES), jnp.float32)]
    return call(functools.partial(col_kernel, len(tiles)), vector(sum(t.shape[1] for t in tiles)), tiles + [side], scratch)


def first_kernel(scaling, a, b0, b1, t0, t1, out):
    step = 2 * LANES

    def multiply(r):
        for b, t in ((b0, t0), (b1, t1)):
            part = lax.dot_general(
                a[r : r + step, :], b[...], (((1,), (1,)), ((), ())), preferred_element_type=jnp.float32
            )
            t[r : r + step, :] = part * scaling

    multiply(0)
    for r in range(0, a.shape[0], step):
        if r + step < a.shape[0]:
            multiply(r + step)
        for at in range(r // LANES, (r + step) // LANES):
            out[at : at + 1, :] = row_lse((t0, t1), None, at)[0]


def first_pass(a, tools, scaling):
    tiles = [jax.ShapeDtypeStruct((a.shape[0], b.shape[0]), jnp.float32) for b in tools]
    flops = 2 * a.size * sum(b.shape[0] for b in tools)
    return call(functools.partial(first_kernel, scaling), tiles + [vector(a.shape[0])], [a] + tools, flops=flops)


def pairs(x, axes):
    return [x, swap(x, axes, 1)]


def by_place(pair, index):
    first = index == 0
    return jnp.stack([jnp.where(first, pair[0], pair[1]), jnp.where(first, pair[1], pair[0])])


def local(queries, tools, query_mass, tool_mass):
    rows = lax.axis_size("row")
    nl = lax.axis_size("zl")
    ri, hi, li, core = (lax.axis_index(a) for a in ("row", "zh", "zl", "core"))
    bq, features = queries.shape
    bt = tools.shape[0]
    scaling = LOG2E / (math.sqrt(features) * EPSILON)

    other_tools = swap(tools, "zh", 1)
    own = swaps(tools, "row")
    half = nl * bq
    firsts = [jnp.full((1,), c * (half // LANES), jnp.int32) for c in (core, 1 - core)]
    held, held_mass, firsts, own[2] = lax.optimization_barrier((queries, tool_mass, firsts, own[2]))
    tile_tools = [place(t, ri).reshape(-1, features) for t in (own, swaps(other_tools, "row"))]
    far, other_mass = swap(held, "zh", 1), swap(held_mass, "zh", 1)
    near_queries = place(swaps(queries, "zl"), li)
    far_queries = place(swaps(far, "zl"), li)
    far_queries, other_mass = lax.optimization_barrier((far_queries, other_mass))
    tile_queries = jnp.stack([near_queries, far_queries])
    tile_queries = jnp.moveaxis(place(pairs(tile_queries, "core"), core, True), 0, 1).reshape(-1, features)
    log_tool = jnp.concatenate([jnp.log2(tool_mass), jnp.log2(other_mass)]).reshape(-1, LANES)
    log_query = jnp.log2(query_mass).reshape(2, nl, 2, bq).transpose(0, 2, 1, 3)
    log_query = by_place([log_query[0], log_query[1]], hi).reshape(-1, LANES)

    *tiles, part = first_pass(tile_queries, tile_tools, scaling)
    for sweep in range(ITERS):
        if sweep:
            (part,) = row_pass(tiles, tool_side, log_query.size)
        got = swaps(part, ("zl", "core"))
        query_side = log_query - lse_of(got[:1] + got[:0:-1])
        got = swaps(col_pass(tiles, query_side), "row")
        tool_side = log_tool - lse_of([got[k] for k in (0, *range(rows - 1, 0, -1))])

    ends = jnp.stack(row_pass(tiles, tool_side, log_query.size // 2, True))
    for axis in (("zl", "core"),):
        got = swaps(ends, axis)
        got = got[:1] + got[:0:-1]
        ends = jnp.stack([lse_of([g[0] for g in got]), functools.reduce(jnp.maximum, [g[1] for g in got])])
    lse, peak = ends

    def mapped_rows(first):
        args = tiles + tile_tools + [tool_side, peak, lse, first]
        flops = 2 * half * tool_side.size * features
        return call(map_kernel, jax.ShapeDtypeStruct((half, features), jnp.float32), args, (), flops, 1)

    others = swap(mapped_rows(firsts[1]), "core", 1).reshape(nl, bq, features)
    own = mapped_rows(firsts[0]).reshape(nl, bq, features)
    own, query_side, tool_side = lax.optimization_barrier((own, query_side, tool_side))
    summed = [pick(own, li ^ k, 0) + pick(others, li ^ k, 0) for k in range(nl)]
    summed = sum([summed[0]] + [swap(summed[k].astype(jnp.float16), "zl", k).astype(jnp.float32) for k in range(1, nl)])
    mapped = summed.astype(jnp.bfloat16)

    unit = EPSILON / LOG2E
    query_potential = query_side.reshape(2, 2, nl, bq).transpose(0, 2, 1, 3)
    query_potential = unit * by_place([query_potential[0], query_potential[1]], hi).reshape(-1)
    return (mapped, query_potential, unit * tool_side.reshape(-1)[: tool_mass.shape[0]])


def solution(mesh):
    rows, cols = mesh.shape["row"], mesh.shape["col"]
    fine = Mesh(mesh.devices.reshape(rows, 2, cols // 4, 2), ("row", "zh", "zl", "core"))
    col = ("zh", "zl", "core")
    in_specs = (P(("row",) + col, None), P(col + ("row",), None), P("row"), P(col))
    out_specs = (P(("row",) + col, None), P("row"), P(col))
    return jax.shard_map(local, mesh=fine, in_specs=in_specs, out_specs=out_specs, check_vma=False)
```
